256 devices in a mesh: cell: 8 (over y, x_lo), gene: 32 (over z, x_hi, core).
Axes of the slice: x: 4 (x_hi: 2, x_lo: 2; x = x_hi * 2 + x_lo), y: 4, z: 8, core: 2. Of those that a mesh axis runs over, the one named last changes fastest.
Arguments:
- counts: float32 [2048, 16384], P('cell', 'gene'), as said below
- gene_mean: float32 [16384], P('gene'), may hold values from -5 to 10
- gene_std: float32 [16384], P('gene'), may hold values from 0 to 10
Outputs:
- gram: float32 [16384, 16384], P('gene', 'cell')
The draws below stay inside these ranges and needn't reach their ends.
Inputs may be any that keep to these rules, and one draw needn't show every extreme that they name: `counts`: whole numbers; every cell has at least one count.
All inputs are finite; a program needn't handle non-finite values.
Results may differ from the reference program's by a relative error of at most 0.013.
Values may be sent and summed in bfloat16 or wider, within the bound.
A program may use at most 128 MiB of HBM per device.

```python
import math
import jax
import jax.numpy as jnp
from jax import lax

GENES = 16384
CELLS = 2048
N_CELL = 8


def raw_counts(key, spread):
    key = jax.random.fold_in(key, 11)
    key_cell, key_gene, key_count, key_pick = jax.random.split(key, 4)
    cell_factor = jnp.exp(jax.random.uniform(key_cell, (CELLS, 1), jnp.float32, -math.log(spread), math.log(spread)))
    ramp = 1.0 + 2.0 * jnp.arange(GENES, dtype=jnp.float32) / GENES
    gene_factor = jnp.exp(jax.random.uniform(key_gene, (1, GENES), jnp.float32, math.log(0.05), math.log(5.0))) * ramp[None, :]
    rate = 0.5 * cell_factor * gene_factor
    counts = jax.random.poisson(key_count, rate).astype(jnp.float32)
    pick = jax.random.randint(key_pick, (CELLS,), 0, GENES)
    extra = (pick[:, None] == jnp.arange(GENES)[None, :]).astype(jnp.float32)
    return counts + extra


def log_stats(key, spread):
    counts = raw_counts(key, spread)
    library = jnp.sum(counts, axis=1, keepdims=True)
    normal = jnp.log1p(counts / library * 10000.0)
    centre = jnp.mean(normal, axis=0)
    deviation = jnp.sqrt(jnp.mean((normal - centre[None, :]) ** 2, axis=0))
    return (centre, deviation)


def draw_counts(key, part):
    spread = 3.0
    counts = raw_counts(key, spread)
    return counts


def draw_gene_mean(key, part):
    spread = 3.0
    centre, deviation = log_stats(key, spread)
    key = jax.random.fold_in(key, 23)
    shift = jax.random.uniform(key, (GENES,), jnp.float32, -0.5, 0.5)
    return (centre + shift * deviation).astype(jnp.float32)


def draw_gene_std(key, part):
    spread = 3.0
    centre, deviation = log_stats(key, spread)
    key = jax.random.fold_in(key, 29)
    factor = jnp.exp(jax.random.uniform(key, (GENES,), jnp.float32, math.log(0.8), math.log(1.25)))
    return (deviation * factor).astype(jnp.float32)


def setup_inputs(seed: int = 0) -> dict:
    keys = jax.random.split(jax.random.key(seed), 4)
    return {
        "counts": draw_counts(jax.random.fold_in(keys[3], 71), 0),
        "gene_mean": draw_gene_mean(jax.random.fold_in(keys[3], 71), 0),
        "gene_std": draw_gene_std(jax.random.fold_in(keys[3], 71), 0),
    }


def standardize(counts, gene_mean, gene_std):
    library = jnp.sum(counts, axis=1, keepdims=True)
    normal = jnp.log1p((counts / library) * 10000.0)
    spread = jnp.maximum(gene_std, 0.1)
    scaled = jnp.minimum((normal - gene_mean[None, :]) / spread[None, :], 10.0)
    return scaled.astype(jnp.bfloat16)


def reference(counts, gene_mean, gene_std):
    scaled = standardize(counts, gene_mean, gene_std)
    blocks = scaled.reshape(N_CELL, CELLS // N_CELL, GENES)

    def add_block(total, block):
        values = block.astype(jnp.float32)
        product = jnp.dot(values.T, values, precision=lax.Precision.HIGHEST)
        rounded = lax.optimization_barrier(product.astype(jnp.bfloat16))
        return total + rounded.astype(jnp.float32), None

    total, _ = lax.scan(add_block, jnp.zeros((GENES, GENES), jnp.float32), blocks)
    return total / CELLS
```

```python
import jax
import jax.numpy as jnp
from jax import lax
from jax.experimental import pallas as pl
from jax.experimental.pallas import tpu as pltpu
from jax.sharding import PartitionSpec as P

MESH = pl.DeviceIdType.MESH
BF16, F32 = jnp.bfloat16, jnp.float32


def kernel(
    counts, mean, std, out,
    raw, part, libs, rows, both, half,
    raw_sem, lib_send, lib_recv, row_send, row_recv, share_send,
    cut_send, cut_recv, ring_send, ring_recv, swap_send, swap_recv, twin_send, twin_recv,
):
    cell, gene = lax.axis_index("cell"), lax.axis_index("gene")
    y, low = cell // 2, cell % 2
    z, high, core = gene // 4, (gene // 2) % 2, gene % 2

    def at(cell_, z_, high_, core_):
        return (cell_, z_ * 4 + high_ * 2 + core_)

    def send(src, dst, send_sem, recv_sem, device):
        return pltpu.make_async_remote_copy(
            src_ref=src,
            dst_ref=dst,
            send_sem=send_sem,
            recv_sem=recv_sem,
            device_id=device,
            device_id_type=MESH,
        )

    fetch = pltpu.make_async_copy(counts, raw, raw_sem)
    fetch.start()

    barrier = pltpu.get_barrier_semaphore()

    def greet(device):
        pl.semaphore_signal(barrier, inc=1, device_id=device, device_id_type=MESH)

    @pl.loop(1, 32)
    def _(off):
        greet((cell, (gene + off) % 32))

    own_chunk = cell == z

    @pl.loop(0, 16)
    def _(n):
        from_high, from_cell = n // 8, n % 8
        itself = own_chunk & (from_high == high) & (from_cell == cell)

        @pl.when(jnp.logical_not(itself))
        def _():
            greet(at(from_cell, cell, from_high, core))

    mirror = y * 2 + (1 - low)
    greet(at(mirror, z, high, core))
    for dy in (1, 2, 3):
        greet(at(((y + dy) % 4) * 2 + low, z, high, core))

    fetch.wait()
    sums = jnp.sum(raw[...], axis=1, keepdims=True)
    part[...] = jnp.broadcast_to(sums, (256, 128)).T[0:1, :]
    libs[gene] = part[...]

    pl.semaphore_wait(barrier, jnp.where(own_chunk, 31 + 15 + 4, 31 + 16 + 4))

    @pl.loop(1, 32)
    def _(off):
        send(
            part, libs.at[gene], lib_send.at[off], lib_recv.at[gene],
            (cell, (gene + off) % 32),
        ).start()

    @pl.loop(1, 32)
    def _(off):
        other = (gene + off) % 32
        send(part, libs.at[other], lib_send.at[off], lib_recv.at[other], (cell, other)).wait_recv()

    total = libs[0]
    for n in range(1, 32):
        total = total + libs[n]
    library = jnp.broadcast_to(total, (128, 256)).T
    library = jnp.concatenate([library] * 4, axis=1)
    normal = jnp.log1p(raw[...] / library * 10000.0)
    spread = jnp.maximum(std[...], 0.1)
    scaled = jnp.minimum((normal - mean[...]) / spread, 10.0).astype(BF16)
    rows[cell] = scaled.reshape(16, 16, 512)

    def cut(j, to_high):
        itself = own_chunk & (j == z) & (to_high == high)
        index = j * 2 + to_high
        device = at(z, j, to_high, core)
        pieces = (
            (rows.at[cell, pl.ds(2 * j, 2), :, pl.ds(0, 256)],
             both.at[core, j, high, :, cell], 0),
            (rows.at[cell, 2 * j + to_high, :, pl.ds(256, 256)],
             half.at[core, j, to_high, high, cell], 1),
        )
        copies = [
            send(src, dst, cut_send.at[n, index], cut_recv.at[n, high, cell], device)
            for src, dst, n in pieces
        ]
        local = [
            pltpu.make_async_copy(src, dst, cut_recv.at[n, high, cell])
            for src, dst, n in pieces
        ]
        return itself, copies, local

    @pl.loop(0, 16)
    def _(n):
        itself, copies, local = cut((z + 4 + n // 2) % 8, n % 2)

        @pl.when(itself)
        def _():
            for copy in local:
                copy.start()

        @pl.when(jnp.logical_not(itself))
        def _():
            for copy in copies:
                copy.start()

    beside = at(mirror, z, high, core)
    along = [((y + dy) % 4) * 2 + low for dy in (1, 3, 2)]
    across = [((y + dy) % 4) * 2 + low for dy in (3, 1, 2)]
    share = send(rows.at[cell], rows.at[cell], share_send, row_recv.at[cell], beside)
    share.start()
    own_rows = [
        send(rows.at[cell], rows.at[cell], row_send.at[0, n], row_recv.at[cell], at(c, z, high, core))
        for n, c in enumerate(along)
    ]
    for copy in own_rows:
        copy.start()

    out[...] = jnp.zeros_like(out)

    @pl.loop(0, 16)
    def _(n):
        from_high, from_cell = n // 8, n % 8
        device = at(from_cell, cell, from_high, core)
        send(
            rows.at[cell, pl.ds(0, 2), :, pl.ds(0, 256)],
            both.at[core, z, from_high, :, from_cell],
            cut_send.at[0, 0], cut_recv.at[0, from_high, from_cell], device,
        ).wait_recv()
        send(
            rows.at[cell, 0, :, pl.ds(256, 256)],
            half.at[core, z, high, from_high, from_cell],
            cut_send.at[1, 0], cut_recv.at[1, from_high, from_cell], device,
        ).wait_recv()

    ahead, behind = at(cell, (z + 1) % 8, high, core), at(cell, (z + 7) % 8, high, core)
    partner = at(cell, z, 1 - high, core)
    twin = at(cell, z, high, 1 - core)
    parts = (("half", 0), ("both", 0), ("half", 1), ("both", 1))

    def piece(kind, side, j):
        return both.at[core, j, side] if kind == "both" else half.at[core, j, high, side]

    def ring(way, hop, n):
        j = (z + 8 - hop if way == 0 else z + hop) % 8
        ref = piece(*parts[n], j)
        return send(ref, ref, ring_send.at[way, hop, n], ring_recv.at[way, hop, n], (ahead, behind)[way])

    def arrival(way, hop, n):
        j = (z + 7 - hop if way == 0 else z + 1 + hop) % 8
        ref = piece(*parts[n], j)
        return send(ref, ref, ring_send.at[way, hop, n], ring_recv.at[way, hop, n], (ahead, behind)[way])

    def place(q):
        return (z + (0, 7, 1, 6, 2, 5, 3, 4)[q]) % 8

    def swap(q, side):
        ref = half.at[core, place(q), high, side]
        return send(ref, ref, swap_send.at[q, side], swap_recv.at[q, side], partner)

    def swapped(q, side):
        ref = half.at[core, place(q), 1 - high, side]
        return send(ref, ref, swap_send.at[q, side], swap_recv.at[q, side], partner)

    def hand(q, kind):
        buf = both if kind == 0 else half
        ref = buf.at[core, place(q)]
        return send(ref, ref, twin_send.at[q, kind], twin_recv.at[q, kind], twin)

    def handed(q, kind):
        buf = both if kind == 0 else half
        ref = buf.at[1 - core, place(q)]
        return send(ref, ref, twin_send.at[q, kind], twin_recv.at[q, kind], twin)

    def finish_swap(q):
        for side in (0, 1):
            swapped(q, side).wait_recv()
        hand(q, 1).start()

    def multiply(q):
        j = place(q)
        handed(q, 0).wait_recv()
        handed(q, 1).wait_recv()
        left = jnp.concatenate(
            [rows[i, 2 * j + t] for t in (0, 1) for i in range(8)], axis=0
        ).T

        @pl.loop(0, 4)
        def _(n):
            side, other = n // 2, n % 2
            right = jnp.concatenate(
                [
                    both[other, j, side].reshape(256, 256),
                    half[other, j, :, side].reshape(256, 256),
                ],
                axis=1,
            )
            columns = pl.ds(pl.multiple_of(n * 512, 512), 512)
            out[:, columns] += jnp.dot(left, right, preferred_element_type=F32)

    for n in range(4):
        ring(0, 0, n).start()
        ring(1, 0, n).start()
        if parts[n][0] == "half":
            swap(0, parts[n][1]).start()
    hand(0, 0).start()

    row_recv_wait = lambda c: send(
        rows.at[c], rows.at[c], share_send, row_recv.at[c], beside
    ).wait_recv()
    row_recv_wait(mirror)
    far_rows = [
        send(rows.at[mirror], rows.at[mirror], row_send.at[1, n], row_recv.at[mirror], at(c, z, high, core))
        for n, c in enumerate(along)
    ]
    for copy in far_rows:
        copy.start()

    for hop in range(4):
        right_q, left_q = 2 * hop + 1, 2 * hop + 2
        for n in range(4):
            kind, side = parts[n]
            for way in (0, 1):
                q = 7 if hop == 3 else (right_q, left_q)[way]
                if hop == 3 and side != way:
                    continue
                arrival(way, hop, n).wait_recv()
                if hop < 2 or (hop == 2 and side == way):
                    ring(way, hop + 1, n).start()
                if kind == "half":
                    swap(q, side).start()
            if n == 2:
                for q in ((0,), (1, 2), (3, 4), (5, 6))[hop]:
                    finish_swap(q)
            if hop == 2:
                if n == 0:
                    for c in across:
                        row_recv_wait(c)
                    for c in across:
                        row_recv_wait(c + 1 - 2 * low)
                    multiply(0)
                if n == 1:
                    multiply(1)
                if n == 2:
                    multiply(2)
        if hop < 3:
            hand(right_q, 0).start()
            hand(left_q, 0).start()
        else:
            hand(7, 0).start()
    multiply(3)
    multiply(4)
    finish_swap(7)
    multiply(5)
    multiply(6)
    multiply(7)

    @pl.loop(1, 32)
    def _(off):
        send(part, libs.at[gene], lib_send.at[off], lib_recv.at[gene], (cell, (gene + off) % 32)).wait_send()

    @pl.loop(0, 16)
    def _(n):
        itself, copies, _ = cut((z + 4 + n // 2) % 8, n % 2)

        @pl.when(jnp.logical_not(itself))
        def _():
            for copy in copies:
                copy.wait_send()

    share.wait_send()
    for copy in own_rows + far_rows:
        copy.wait_send()
    for way in (0, 1):
        for hop in range(4):
            for n in range(4):
                if hop < 3 or parts[n][1] == way:
                    ring(way, hop, n).wait_send()
    for q in range(8):
        for side in (0, 1):
            swap(q, side).wait_send()
            hand(q, side).wait_send()


def shards(counts, gene_mean, gene_std):
    dma = pltpu.SemaphoreType.DMA
    gram = pl.pallas_call(
        kernel,
        out_shape=jax.ShapeDtypeStruct((512, 2048), F32),
        in_specs=[
            pl.BlockSpec(memory_space=pl.ANY),
            pl.BlockSpec(memory_space=pltpu.VMEM),
            pl.BlockSpec(memory_space=pltpu.VMEM),
        ],
        out_specs=pl.BlockSpec(memory_space=pltpu.VMEM),
        scratch_shapes=[
            pltpu.VMEM((256, 512), F32),
            pltpu.VMEM((1, 256), F32),
            pltpu.VMEM((32, 1, 256), F32),
            pltpu.VMEM((8, 16, 16, 512), BF16),
            pltpu.VMEM((2, 8, 2, 2, 8, 16, 256), BF16),
            pltpu.VMEM((2, 8, 2, 2, 8, 16, 256), BF16),
            dma,
            dma((32,)),
            dma((32,)),
            dma((2, 3)),
            dma((8,)),
            dma,
            dma((2, 16)),
            dma((2, 2, 8)),
            dma((2, 4, 4)),
            dma((2, 4, 4)),
            dma((8, 2)),
            dma((8, 2)),
            dma((8, 2)),
            dma((8, 2)),
        ],
        compiler_params=pltpu.CompilerParams(
            collective_id=0, has_side_effects=True, vmem_limit_bytes=40 << 20
        ),
        cost_estimate=pl.CostEstimate(
            flops=2 * 512 * 2048 * 2048, bytes_accessed=5 << 20, transcendentals=1 << 17
        ),
    )(counts, gene_mean.reshape(1, 512), gene_std.reshape(1, 512))
    return gram * (1.0 / 2048)


def solution(mesh):
    placed = (P("cell", "gene"), P("gene"), P("gene"))
    return jax.shard_map(
        shards, mesh=mesh, in_specs=placed, out_specs=P("gene", "cell"), check_vma=False
    )
```

```python
import jax
import jax.numpy as jnp
from jax import lax
from jax.experimental import pallas as pl
from jax.experimental.pallas import tpu as pltpu
from jax.sharding import PartitionSpec as P

MESH = pl.DeviceIdType.MESH
BF16, F32 = jnp.bfloat16, jnp.float32
SHARED = (256, 256)
PLACES = (0, 7, 1, 6, 2, 5, 3, 4)


def kernel(
    counts, mean, std, out,
    raw, centre, width, part, libs, rows, cols, lhs,
    raw_sem, lib_send, lib_recv, row_send, row_recv, cut_send, cut_recv,
    ring_send, ring_recv, swap_send, swap_recv, twin_send, twin_recv,
):
    cell, gene = lax.axis_index("cell"), lax.axis_index("gene")
    y, low = cell // 2, cell % 2
    z, high, core = gene // 4, (gene // 2) % 2, gene % 2
    other = 1 - high

    def at(cell_, z_, high_, core_):
        return (cell_, z_ * 4 + high_ * 2 + core_)

    def send(src, dst, send_sem, recv_sem, device):
        return pltpu.make_async_remote_copy(
            src_ref=src,
            dst_ref=dst,
            send_sem=send_sem,
            recv_sem=recv_sem,
            device_id=device,
            device_id_type=MESH,
        )

    ahead, behind = at(cell, (z + 1) % 8, high, core), at(cell, (z + 7) % 8, high, core)
    partner, twin = at(cell, z, other, core), at(cell, z, high, 1 - core)
    mirror = y * 2 + (1 - low)
    own_plane = cell == z

    fetches = [
        pltpu.make_async_copy(counts, raw, raw_sem.at[0]),
        pltpu.make_async_copy(mean, centre, raw_sem.at[1]),
        pltpu.make_async_copy(std, width, raw_sem.at[2]),
    ]
    for fetch in fetches:
        fetch.start()

    barrier = pltpu.get_barrier_semaphore()

    def greet(device):
        pl.semaphore_signal(barrier, inc=1, device_id=device, device_id_type=MESH)

    @pl.loop(0, 8)
    def _(n):
        @pl.when(jnp.logical_not(own_plane & (n == cell)))
        def _():
            greet(at(n, cell, high, core))

    def far_first(n):
        return 16 + ((n + 1) // 2) * (1 - 2 * (n % 2))

    @pl.loop(0, 31)
    def _(n):
        greet((cell, (gene + far_first(n)) % 32))

    greet(at(mirror, z, high, core))
    for dy in (1, 2, 3):
        greet(at(((y + dy) % 4) * 2 + low, z, high, core))

    for fetch in fetches:
        fetch.wait()
    sums = jnp.sum(raw[...], axis=1, keepdims=True)
    part[...] = jnp.broadcast_to(sums, (256, 128)).T[0:1, :]
    libs[gene] = part[...]

    pl.semaphore_wait(barrier, jnp.where(own_plane, 7 + 31 + 4, 8 + 31 + 4))

    def total_to(off):
        to = (gene + off) % 32
        return send(part, libs.at[gene], lib_send.at[off], lib_recv.at[gene], (cell, to))

    def total_from(off):
        of = (gene + off) % 32
        return send(part, libs.at[of], lib_send.at[off], lib_recv.at[of], (cell, of))

    @pl.loop(0, 31)
    def _(n):
        total_to(far_first(n)).start()

    @pl.loop(1, 32)
    def _(off):
        total_from(off).wait_recv()

    total = libs[0]
    for n in range(1, 32):
        total = total + libs[n]
    def lanes(kind, side):
        shared = SHARED[side]
        return pl.ds(shared, 512 - shared) if kind == 0 else pl.ds(0, shared)

    def cut(j, kind, side):
        return send(
            rows.at[cell, j, :, lanes(kind, side)],
            cols.at[core, j, high, cell, :, lanes(kind, side)],
            cut_send.at[kind, j],
            cut_recv.at[kind, cell],
            at(z, j, high, core),
        )

    def cut_local(j, kind, side):
        return pltpu.make_async_copy(
            rows.at[cell, j, :, lanes(kind, side)],
            cols.at[core, j, high, cell, :, lanes(kind, side)],
            cut_recv.at[kind, cell],
        )

    def cut_from(i, kind, side):
        return send(
            rows.at[cell, z, :, lanes(kind, side)],
            cols.at[core, z, high, i, :, lanes(kind, side)],
            cut_send.at[kind, z],
            cut_recv.at[kind, i],
            at(i, cell, high, core),
        )

    def cut_all(kind, side, local, remote):
        @pl.loop(0, 8)
        def _(n):
            j = (z + 4 + n) % 8
            itself = own_plane & (j == z)
            if local:

                @pl.when(itself)
                def _():
                    cut_local(j, kind, side).start()

            @pl.when(jnp.logical_not(itself))
            def _():
                remote(cut(j, kind, side))

    def on_side(side):
        return (cell // 4) == side

    factor = jnp.broadcast_to(10000.0 / total, (128, 256)).T
    inverse = 1.0 / jnp.maximum(width[...], 0.1)

    def standardize(first, last):
        factors = jnp.concatenate([factor] * ((last - first) // 128), axis=1)
        normal = jnp.log1p(raw[:, first:last] * factors)
        scaled = jnp.minimum((normal - centre[:, first:last]) * inverse[:, first:last], 10.0)
        rows[cell, :, :, first:last] = scaled.astype(BF16).reshape(8, 32, last - first)

    split = min(SHARED)
    for kind in (0, 1):
        if kind == 0:
            standardize(split, 512)
        else:
            standardize(0, split)
        if SHARED[0] == SHARED[1]:
            cut_all(kind, 0, True, lambda copy: copy.start())
        else:
            for side in (0, 1):

                @pl.when(on_side(side))
                def _():
                    cut_all(kind, side, True, lambda copy: copy.start())

    along = [((y + dy) % 4) * 2 + low for dy in (1, 3, 2)]

    def row_to(n, whose, target):
        return send(
            rows.at[whose], rows.at[whose], row_send.at[n], row_recv.at[whose],
            at(target, z, high, core),
        )

    row_copies = [row_to(0, cell, mirror)] + [
        row_to(1 + n, cell, c) for n, c in enumerate(along)
    ]
    for copy in row_copies:
        copy.start()

    out[...] = jnp.zeros_like(out)

    parts = [(s, k, side) for s, k in ((0, 0), (0, 1), (1, 1)) for side in (0, 1)]

    def place(q):
        return (z + PLACES[q]) % 8

    def view(j, whose, kind, side):
        return cols.at[core, j, whose, pl.ds(4 * side, 4), :, lanes(kind, side)]

    def piece(n, j):
        s, kind, side = parts[n]
        return view(j, other if s else high, kind, side)

    def ring(way, hop, n, j):
        ref = piece(n, j)
        return send(
            ref, ref, ring_send.at[way, hop, n], ring_recv.at[way, hop, n],
            (ahead, behind)[way],
        )

    def onward(way, hop, n):
        return ring(way, hop, n, (z + 8 - hop if way == 0 else z + hop) % 8)

    def arrival(way, hop, n):
        return ring(way, hop, n, (z + 7 - hop if way == 0 else z + 1 + hop) % 8)

    def swap(q, kind, side):
        ref = view(place(q), high, kind, side)
        return send(ref, ref, swap_send.at[kind, q, side], swap_recv.at[kind, q, side], partner)

    def swapped(q, kind, side):
        ref = view(place(q), other, kind, side)
        return send(ref, ref, swap_send.at[kind, q, side], swap_recv.at[kind, q, side], partner)

    def hand(q, s):
        ref = cols.at[core, place(q), other if s else high]
        return send(ref, ref, twin_send.at[q, s], twin_recv.at[q, s], twin)

    def handed(q, s):
        ref = cols.at[1 - core, place(q), other if s else high]
        return send(ref, ref, twin_send.at[q, s], twin_recv.at[q, s], twin)

    def finish(q):
        for side in (0, 1):
            swapped(q, 0, side).wait_recv()
        hand(q, 1).start()

    def prepare(q):
        j = place(q)
        lhs[...] = jnp.concatenate([rows[i, j] for i in range(8)], axis=0).T

    def product(q, s, own):
        j, whose, which = place(q), other if s else high, core if own else 1 - core
        right = cols[which, j, whose].reshape(256, 512)
        columns = pl.ds(pl.multiple_of((whose * 2 + which) * 512, 512), 512)
        out[:, columns] += jnp.dot(lhs[...], right, preferred_element_type=F32)

    def multiply(q):
        handed(q, 0).wait_recv()
        handed(q, 1).wait_recv()
        prepare(q)
        j = place(q)

        @pl.loop(0, 4)
        def _(n):
            right = cols[n % 2, j, n // 2].reshape(256, 512)
            columns = pl.ds(pl.multiple_of(n * 512, 512), 512)
            out[:, columns] += jnp.dot(lhs[...], right, preferred_element_type=F32)

    for kind in (0, 1):
        for side in (0, 1):
            for i in range(4 * side, 4 * side + 4):
                cut_from(i, kind, side).wait_recv()
            for way in (0, 1):
                onward(way, 0, 2 * kind + side).start()
            swap(0, kind, side).start()
    hand(0, 0).start()
    row_to(0, mirror, mirror).wait_recv()
    far_copies = [row_to(4 + n, mirror, c) for n, c in enumerate(along)]
    for copy in far_copies:
        copy.start()
    for side in (0, 1):
        swapped(0, 1, side).wait_recv()
        for way in (0, 1):
            onward(way, 0, 4 + side).start()
    finish(0)

    @pl.loop(1, 32)
    def _(off):
        total_to(off).wait_send()

    def rows_arrive():
        for dy in (1, 2, 3):
            for l in (0, 1):
                c = ((y + dy) % 4) * 2 + l
                row_to(0, c, mirror).wait_recv()

    def cuts_left():
        for kind in (0, 1):
            if SHARED[0] == SHARED[1]:
                cut_all(kind, 0, False, lambda copy: copy.wait_send())
            else:
                for side in (0, 1):

                    @pl.when(on_side(side))
                    def _():
                        cut_all(kind, side, False, lambda copy: copy.wait_send())

    def rows_left():
        for copy in row_copies + far_copies:
            copy.wait_send()

    def ring_left(hop):
        for way in (0, 1):
            for n in range(6):
                if hop < 3 or parts[n][2] == way:
                    onward(way, hop, n).wait_send()

    def swaps_left(q):
        for side in (0, 1):
            swap(q, 0, side).wait_send()
            hand(q, side).wait_send()

    beside = {
        (0, 3): [cuts_left],
        (1, 1): [lambda: finish(1)],
        (1, 3): [lambda: finish(2)],
        (1, 5): [lambda: ring_left(0)],
        (2, 0): [rows_arrive, lambda: multiply(0)],
        (2, 1): [lambda: multiply(1), lambda: finish(3)],
        (2, 2): [lambda: multiply(2), lambda: finish(4)],
        (2, 3): [rows_left, lambda: ring_left(1)],
        (2, 4): [lambda: multiply(3)],
        (2, 5): [lambda: multiply(4)],
        (3, 1): [lambda: finish(5), lambda: finish(6)],
        (3, 3): [lambda: multiply(5), lambda: multiply(6), lambda: ring_left(2), lambda: prepare(7)],
    }
    for hop in range(4):
        for n in range(6):
            s, kind, side = parts[n]
            for way in (0, 1):
                if hop == 3 and side != way:
                    continue
                arrival(way, hop, n).wait_recv()
                if hop < 2 or (hop == 2 and side == way):
                    onward(way, hop + 1, n).start()
                q = 7 if hop == 3 else 2 * hop + 1 + way
                if (s, kind) == (0, 0):
                    swap(q, 0, side).start()
                if n == 3 and hop < 3:
                    hand(q, 0).start()
            if n == 3 and hop == 3:
                hand(7, 0).start()
            for action in beside.get((hop, n), ()):
                action()
    product(7, 0, True)
    handed(7, 0).wait_recv()
    finish(7)
    product(7, 0, False)
    product(7, 1, True)
    handed(7, 1).wait_recv()
    product(7, 1, False)

    for side in (0, 1):
        swap(0, 1, side).wait_send()
    for q in range(8):
        swaps_left(q)
    ring_left(3)


def shards(counts, gene_mean, gene_std):
    dma = pltpu.SemaphoreType.DMA
    operands = counts, gene_mean.reshape(1, 512), gene_std.reshape(1, 512)
    operands = [pltpu.with_memory_space_constraint(a, pltpu.HBM) for a in operands]
    gram = pl.pallas_call(
        kernel,
        out_shape=jax.ShapeDtypeStruct((512, 2048), F32),
        in_specs=[pl.BlockSpec(memory_space=pltpu.HBM)] * 3,
        out_specs=pl.BlockSpec(memory_space=pltpu.VMEM),
        scratch_shapes=[
            pltpu.VMEM((256, 512), F32),
            pltpu.VMEM((1, 512), F32),
            pltpu.VMEM((1, 512), F32),
            pltpu.VMEM((1, 256), F32),
            pltpu.VMEM((32, 1, 256), F32),
            pltpu.VMEM((8, 8, 32, 512), BF16),
            pltpu.VMEM((2, 8, 2, 8, 32, 512), BF16),
            pltpu.VMEM((512, 256), BF16),
            dma((3,)),
            dma((32,)),
            dma((32,)),
            dma((7,)),
            dma((8,)),
            dma((2, 8)),
            dma((2, 8)),
            dma((2, 4, 6)),
            dma((2, 4, 6)),
            dma((2, 8, 2)),
            dma((2, 8, 2)),
            dma((8, 2)),
            dma((8, 2)),
        ],
        compiler_params=pltpu.CompilerParams(
            collective_id=0, has_side_effects=True, vmem_limit_bytes=40 << 20
        ),
        cost_estimate=pl.CostEstimate(
            flops=2 * 512 * 2048 * 2048, bytes_accessed=5 << 20, transcendentals=1 << 17
        ),
    )(*operands)
    return gram * (1.0 / 2048)


def solution(mesh):
    placed = (P("cell", "gene"), P("gene"), P("gene"))
    return jax.shard_map(
        shards, mesh=mesh, in_specs=placed, out_specs=P("gene", "cell"), check_vma=False
    )
```

```python
import jax
import jax.numpy as jnp
from jax import lax
from jax.experimental import pallas as pl
from jax.experimental.pallas import tpu as pltpu
from jax.sharding import PartitionSpec as P

MESH = pl.DeviceIdType.MESH
BF16, F32 = jnp.bfloat16, jnp.float32
SHARED = (256, 256)
PLACES = (0, 7, 1, 6, 2, 5, 3, 4)


def kernel(
    counts, mean, std, out,
    raw, centre, width, part, libs, rows, cols, lhs,
    raw_sem, lib_send, lib_recv, row_send, row_recv, cut_send, cut_recv,
    ring_send, ring_recv, swap_send, swap_recv, twin_send, twin_recv, last_send, last_recv,
):
    cell, gene = lax.axis_index("cell"), lax.axis_index("gene")
    y, low = cell // 2, cell % 2
    z, high, core = gene // 4, (gene // 2) % 2, gene % 2
    other = 1 - high

    def at(cell_, z_, high_, core_):
        return (cell_, z_ * 4 + high_ * 2 + core_)

    def send(src, dst, send_sem, recv_sem, device):
        return pltpu.make_async_remote_copy(
            src_ref=src,
            dst_ref=dst,
            send_sem=send_sem,
            recv_sem=recv_sem,
            device_id=device,
            device_id_type=MESH,
        )

    ahead, behind = at(cell, (z + 1) % 8, high, core), at(cell, (z + 7) % 8, high, core)
    partner, twin = at(cell, z, other, core), at(cell, z, high, 1 - core)
    mirror = y * 2 + (1 - low)
    own_plane = cell == z

    fetches = [
        pltpu.make_async_copy(counts, raw, raw_sem.at[0]),
        pltpu.make_async_copy(mean, centre, raw_sem.at[1]),
        pltpu.make_async_copy(std, width, raw_sem.at[2]),
    ]
    for fetch in fetches:
        fetch.start()

    barrier = pltpu.get_barrier_semaphore()

    def greet(device):
        pl.semaphore_signal(barrier, inc=1, device_id=device, device_id_type=MESH)

    @pl.loop(0, 8)
    def _(n):
        @pl.when(jnp.logical_not(own_plane & (n == cell)))
        def _():
            greet(at(n, cell, high, core))

    def far_first(n):
        return 16 + ((n + 1) // 2) * (1 - 2 * (n % 2))

    @pl.loop(0, 31)
    def _(n):
        greet((cell, (gene + far_first(n)) % 32))

    greet(at(mirror, z, high, core))
    for dy in (1, 2, 3):
        greet(at(((y + dy) % 4) * 2 + low, z, high, core))

    for fetch in fetches:
        fetch.wait()
    sums = jnp.sum(raw[...], axis=1, keepdims=True)
    part[...] = jnp.broadcast_to(sums, (256, 128)).T[0:1, :]
    libs[gene] = part[...]

    pl.semaphore_wait(barrier, jnp.where(own_plane, 7 + 31 + 4, 8 + 31 + 4))

    def total_to(off):
        to = (gene + off) % 32
        return send(part, libs.at[gene], lib_send.at[off], lib_recv.at[gene], (cell, to))

    def total_from(off):
        of = (gene + off) % 32
        return send(part, libs.at[of], lib_send.at[off], lib_recv.at[of], (cell, of))

    @pl.loop(0, 31)
    def _(n):
        total_to(far_first(n)).start()

    @pl.loop(1, 32)
    def _(off):
        total_from(off).wait_recv()

    total = libs[0]
    for n in range(1, 32):
        total = total + libs[n]
    def lanes(kind, side):
        shared = SHARED[side]
        return pl.ds(shared, 512 - shared) if kind == 0 else pl.ds(0, shared)

    def cut(j, kind, side):
        return send(
            rows.at[cell, j, :, lanes(kind, side)],
            cols.at[core, j, high, cell, :, lanes(kind, side)],
            cut_send.at[kind, j],
            cut_recv.at[kind, cell],
            at(z, j, high, core),
        )

    def cut_local(j, kind, side):
        return pltpu.make_async_copy(
            rows.at[cell, j, :, lanes(kind, side)],
            cols.at[core, j, high, cell, :, lanes(kind, side)],
            cut_recv.at[kind, cell],
        )

    def cut_from(i, kind, side):
        return send(
            rows.at[cell, z, :, lanes(kind, side)],
            cols.at[core, z, high, i, :, lanes(kind, side)],
            cut_send.at[kind, z],
            cut_recv.at[kind, i],
            at(i, cell, high, core),
        )

    def cut_all(kind, side, local, remote):
        @pl.loop(0, 8)
        def _(n):
            j = (z + 4 + n) % 8
            itself = own_plane & (j == z)
            if local:

                @pl.when(itself)
                def _():
                    cut_local(j, kind, side).start()

            @pl.when(jnp.logical_not(itself))
            def _():
                remote(cut(j, kind, side))

    def on_side(side):
        return (cell // 4) == side

    factor = jnp.broadcast_to(10000.0 / total, (128, 256)).T
    inverse = 1.0 / jnp.maximum(width[...], 0.1)

    def standardize(first, last):
        factors = jnp.concatenate([factor] * ((last - first) // 128), axis=1)
        normal = jnp.log1p(raw[:, first:last] * factors)
        scaled = jnp.minimum((normal - centre[:, first:last]) * inverse[:, first:last], 10.0)
        rows[cell, :, :, first:last] = scaled.astype(BF16).reshape(8, 32, last - first)

    split = min(SHARED)
    for kind in (0, 1):
        if kind == 0:
            standardize(split, 512)
        else:
            standardize(0, split)
        if SHARED[0] == SHARED[1]:
            cut_all(kind, 0, True, lambda copy: copy.start())
        else:
            for side in (0, 1):

                @pl.when(on_side(side))
                def _():
                    cut_all(kind, side, True, lambda copy: copy.start())

    along = [((y + dy) % 4) * 2 + low for dy in (1, 3, 2)]

    def row_to(n, whose, target):
        return send(
            rows.at[whose], rows.at[whose], row_send.at[n], row_recv.at[whose],
            at(target, z, high, core),
        )

    row_copies = [row_to(0, cell, mirror)] + [
        row_to(1 + n, cell, c) for n, c in enumerate(along)
    ]
    for copy in row_copies:
        copy.start()

    out[...] = jnp.zeros_like(out)

    parts = [(s, k, side) for s, k in ((0, 0), (0, 1), (1, 1)) for side in (0, 1)]

    def place(q):
        return (z + PLACES[q]) % 8

    def view(j, whose, kind, side):
        return cols.at[core, j, whose, pl.ds(4 * side, 4), :, lanes(kind, side)]

    def piece(n, j):
        s, kind, side = parts[n]
        return view(j, other if s else high, kind, side)

    def ring(way, hop, n, j):
        ref = piece(n, j)
        return send(
            ref, ref, ring_send.at[way, hop, n], ring_recv.at[way, hop, n],
            (ahead, behind)[way],
        )

    def onward(way, hop, n):
        return ring(way, hop, n, (z + 8 - hop if way == 0 else z + hop) % 8)

    def arrival(way, hop, n):
        return ring(way, hop, n, (z + 7 - hop if way == 0 else z + 1 + hop) % 8)

    def swap(q, kind, side):
        ref = view(place(q), high, kind, side)
        return send(ref, ref, swap_send.at[kind, q, side], swap_recv.at[kind, q, side], partner)

    def swapped(q, kind, side):
        ref = view(place(q), other, kind, side)
        return send(ref, ref, swap_send.at[kind, q, side], swap_recv.at[kind, q, side], partner)

    def hand(q, s):
        ref = cols.at[core, place(q), other if s else high]
        return send(ref, ref, twin_send.at[q, s], twin_recv.at[q, s], twin)

    def handed(q, s):
        ref = cols.at[1 - core, place(q), other if s else high]
        return send(ref, ref, twin_send.at[q, s], twin_recv.at[q, s], twin)

    def last_hand(kind, side):
        ref = view(place(7), other, kind, side)
        return send(ref, ref, last_send.at[kind, side], last_recv.at[kind, side], twin)

    def last_handed(kind, side):
        ref = cols.at[1 - core, place(7), other, pl.ds(4 * side, 4), :, lanes(kind, side)]
        return send(ref, ref, last_send.at[kind, side], last_recv.at[kind, side], twin)

    def finish(q):
        for side in (0, 1):
            swapped(q, 0, side).wait_recv()
        hand(q, 1).start()

    def prepare(*qs):
        for q in qs:
            j = place(q)
            lhs[q] = jnp.concatenate([rows[i, j] for i in range(8)], axis=0).T

    def product(q, s, own, first=0, last=512):
        j, whose, which = place(q), other if s else high, core if own else 1 - core
        right = cols[which, j, whose, :, :, first:last].reshape(256, last - first)
        start = pl.multiple_of((whose * 2 + which) * 512 + first, 128)
        columns = pl.ds(start, last - first)
        out[:, columns] += jnp.dot(lhs[q], right, preferred_element_type=F32)

    def multiply(s, *qs):
        for q in qs:
            handed(q, s).wait_recv()
        whose = other if s else high

        @pl.loop(0, 2)
        def _(which):
            columns = pl.ds(pl.multiple_of((whose * 2 + which) * 512, 512), 512)
            right = [cols[which, place(q), whose].reshape(256, 512) for q in qs]
            left = [lhs[q] for q in qs]
            if len(qs) > 1:
                left, right = jnp.concatenate(left, axis=1), jnp.concatenate(right, axis=0)
            else:
                left, right = left[0], right[0]
            out[:, columns] += jnp.dot(left, right, preferred_element_type=F32)

    for kind in (0, 1):
        for side in (0, 1):
            for i in range(4 * side, 4 * side + 4):
                cut_from(i, kind, side).wait_recv()
            for way in (0, 1):
                onward(way, 0, 2 * kind + side).start()
            swap(0, kind, side).start()
    hand(0, 0).start()
    row_to(0, mirror, mirror).wait_recv()
    far_copies = [row_to(4 + n, mirror, c) for n, c in enumerate(along)]
    for copy in far_copies:
        copy.start()

    def begin_shared():
        for side in (0, 1):
            swapped(0, 1, side).wait_recv()
            for way in (0, 1):
                onward(way, 0, 4 + side).start()
        finish(0)

    def totals_left():
        @pl.loop(1, 32)
        def _(off):
            total_to(off).wait_send()

    def rows_arrive():
        for dy in (1, 2, 3):
            for l in (0, 1):
                c = ((y + dy) % 4) * 2 + l
                row_to(0, c, mirror).wait_recv()

    def cuts_left():
        for kind in (0, 1):
            if SHARED[0] == SHARED[1]:
                cut_all(kind, 0, False, lambda copy: copy.wait_send())
            else:
                for side in (0, 1):

                    @pl.when(on_side(side))
                    def _():
                        cut_all(kind, side, False, lambda copy: copy.wait_send())

    def rows_left():
        for copy in row_copies + far_copies:
            copy.wait_send()

    def ring_left(hop):
        for way in (0, 1):
            for n in range(6):
                if hop < 3 or parts[n][2] == way:
                    onward(way, hop, n).wait_send()

    def swaps_left(q):
        for side in (0, 1):
            swap(q, 0, side).wait_send()
        hand(q, 0).wait_send()
        if q < 7:
            hand(q, 1).wait_send()

    def last_swapped():
        for side in (0, 1):
            swapped(7, 0, side).wait_recv()
            last_hand(0, side).start()
        product(7, 0, True)
        product(7, 1, True, wide, 512)

    wide = max(SHARED)
    beside = {
        (0, 0): [begin_shared],
        (1, 0): [cuts_left],
        (2, 0): [lambda: finish(1), lambda: finish(2)],
        (1, 1): [totals_left],
        (2, 1): [lambda: finish(3), lambda: finish(4), rows_arrive, lambda: prepare(0, 1, 2), lambda: multiply(0, 0, 1, 2)],
        (1, 2): [lambda: multiply(1, 0, 1, 2), lambda: prepare(3, 4)],
        (0, 3): [lambda: multiply(0, 3, 4), lambda: multiply(1, 3, 4), lambda: prepare(5, 6, 7)],
        (2, 2): [lambda: finish(5), lambda: finish(6), lambda: multiply(0, 5, 6), lambda: ring_left(0), rows_left],
        (1, 3): [lambda: multiply(1, 5, 6), last_swapped],
    }
    order = (
        (0, 0), (1, 0), (0, 1), (2, 0), (1, 1), (0, 2),
        (2, 1), (1, 2), (0, 3), (2, 2), (1, 3), (2, 3),
    )
    for p, hop in order:
        for side in (0, 1):
            n = 2 * p + side
            for way in (0, 1):
                if hop == 3 and side != way:
                    continue
                arrival(way, hop, n).wait_recv()
                if hop < 2 or (hop == 2 and side == way):
                    onward(way, hop + 1, n).start()
                if p == 0:
                    swap(7 if hop == 3 else 2 * hop + 1 + way, 0, side).start()
                if (p, hop) == (2, 3):
                    last_hand(1, side).start()
        if p == 1:
            for q in (7,) if hop == 3 else (2 * hop + 1, 2 * hop + 2):
                hand(q, 0).start()
        for action in beside.get((p, hop), ()):
            action()
    product(7, 1, True, 0, wide)
    handed(7, 0).wait_recv()
    product(7, 0, False)
    for side in (0, 1):
        last_handed(0, side).wait_recv()
    product(7, 1, False, wide, 512)
    for side in (0, 1):
        last_handed(1, side).wait_recv()
    product(7, 1, False, 0, wide)

    for kind in (0, 1):
        for side in (0, 1):
            last_hand(kind, side).wait_send()
    for side in (0, 1):
        swap(0, 1, side).wait_send()
    for q in range(8):
        swaps_left(q)
    for hop in (1, 2, 3):
        ring_left(hop)


def shards(counts, gene_mean, gene_std):
    dma = pltpu.SemaphoreType.DMA
    operands = counts, gene_mean.reshape(1, 512), gene_std.reshape(1, 512)
    operands = [pltpu.with_memory_space_constraint(a, pltpu.HBM) for a in operands]
    gram = pl.pallas_call(
        kernel,
        out_shape=jax.ShapeDtypeStruct((512, 2048), F32),
        in_specs=[pl.BlockSpec(memory_space=pltpu.HBM)] * 3,
        out_specs=pl.BlockSpec(memory_space=pltpu.VMEM),
        scratch_shapes=[
            pltpu.VMEM((256, 512), F32),
            pltpu.VMEM((1, 512), F32),
            pltpu.VMEM((1, 512), F32),
            pltpu.VMEM((1, 256), F32),
            pltpu.VMEM((32, 1, 256), F32),
            pltpu.VMEM((8, 8, 32, 512), BF16),
            pltpu.VMEM((2, 8, 2, 8, 32, 512), BF16),
            pltpu.VMEM((8, 512, 256), BF16),
            dma((3,)),
            dma((32,)),
            dma((32,)),
            dma((7,)),
            dma((8,)),
            dma((2, 8)),
            dma((2, 8)),
            dma((2, 4, 6)),
            dma((2, 4, 6)),
            dma((2, 8, 2)),
            dma((2, 8, 2)),
            dma((8, 2)),
            dma((8, 2)),
            dma((2, 2)),
            dma((2, 2)),
        ],
        compiler_params=pltpu.CompilerParams(
            collective_id=0, has_side_effects=True, vmem_limit_bytes=40 << 20
        ),
        cost_estimate=pl.CostEstimate(
            flops=2 * 512 * 2048 * 2048, bytes_accessed=5 << 20, transcendentals=1 << 17
        ),
    )(*operands)
    return gram * (1.0 / 2048)


def solution(mesh):
    placed = (P("cell", "gene"), P("gene"), P("gene"))
    return jax.shard_map(
        shards, mesh=mesh, in_specs=placed, out_specs=P("gene", "cell"), check_vma=False
    )
```

```python
import jax
import jax.numpy as jnp
from jax import lax
from jax.experimental import pallas as pl
from jax.experimental.pallas import tpu as pltpu
from jax.sharding import PartitionSpec as P

MESH = pl.DeviceIdType.MESH
BF16, F32 = jnp.bfloat16, jnp.float32
SHARED = (256, 256)
PLACES = (0, 7, 1, 6, 2, 5, 3, 4)


def kernel(
    counts, mean, std, out,
    raw, centre, width, part, libs, rows, cols, lhs,
    raw_sem, lib_send, lib_recv, row_send, row_recv, cut_send, cut_recv,
    ring_send, ring_recv, swap_send, swap_recv, twin_send, twin_recv, last_send, last_recv,
):
    cell, gene = lax.axis_index("cell"), lax.axis_index("gene")
    y, low = cell // 2, cell % 2
    z, high, core = gene // 4, (gene // 2) % 2, gene % 2
    other = 1 - high

    def at(cell_, z_, high_, core_):
        return (cell_, z_ * 4 + high_ * 2 + core_)

    def send(src, dst, send_sem, recv_sem, device):
        return pltpu.make_async_remote_copy(
            src_ref=src,
            dst_ref=dst,
            send_sem=send_sem,
            recv_sem=recv_sem,
            device_id=device,
            device_id_type=MESH,
        )

    ahead, behind = at(cell, (z + 1) % 8, high, core), at(cell, (z + 7) % 8, high, core)
    partner, twin = at(cell, z, other, core), at(cell, z, high, 1 - core)
    mirror = y * 2 + (1 - low)
    own_plane = cell == z

    fetches = [
        pltpu.make_async_copy(counts, raw, raw_sem.at[0]),
        pltpu.make_async_copy(mean, centre, raw_sem.at[1]),
        pltpu.make_async_copy(std, width, raw_sem.at[2]),
    ]
    for fetch in fetches:
        fetch.start()

    barrier = pltpu.get_barrier_semaphore()

    def greet(device):
        pl.semaphore_signal(barrier, inc=1, device_id=device, device_id_type=MESH)

    @pl.loop(0, 8)
    def _(n):
        @pl.when(jnp.logical_not(own_plane & (n == cell)))
        def _():
            greet(at(n, cell, high, core))

    def far_first(n):
        return 16 + ((n + 1) // 2) * (1 - 2 * (n % 2))

    @pl.loop(0, 31)
    def _(n):
        greet((cell, (gene + far_first(n)) % 32))

    greet(at(mirror, z, high, core))
    for dy in (1, 2, 3):
        greet(at(((y + dy) % 4) * 2 + low, z, high, core))

    for fetch in fetches:
        fetch.wait()
    sums = jnp.sum(raw[...], axis=1, keepdims=True)
    part[...] = jnp.broadcast_to(sums, (256, 128)).T[0:1, :]
    libs[gene] = part[...]

    pl.semaphore_wait(barrier, jnp.where(own_plane, 7 + 31 + 4, 8 + 31 + 4))

    def total_to(off):
        to = (gene + off) % 32
        return send(part, libs.at[gene], lib_send.at[off], lib_recv.at[gene], (cell, to))

    def total_from(off):
        of = (gene + off) % 32
        return send(part, libs.at[of], lib_send.at[off], lib_recv.at[of], (cell, of))

    @pl.loop(0, 31)
    def _(n):
        total_to(far_first(n)).start()

    @pl.loop(1, 32)
    def _(off):
        total_from(off).wait_recv()

    total = libs[0]
    for n in range(1, 32):
        total = total + libs[n]
    def lanes(kind, side):
        shared = SHARED[side]
        return pl.ds(shared, 512 - shared) if kind == 0 else pl.ds(0, shared)

    def cut(j, kind, side):
        return send(
            rows.at[cell, j, :, lanes(kind, side)],
            cols.at[core, j, high, cell, :, lanes(kind, side)],
            cut_send.at[kind, j],
            cut_recv.at[kind, cell],
            at(z, j, high, core),
        )

    def cut_local(j, kind, side):
        return pltpu.make_async_copy(
            rows.at[cell, j, :, lanes(kind, side)],
            cols.at[core, j, high, cell, :, lanes(kind, side)],
            cut_recv.at[kind, cell],
        )

    def cut_from(i, kind, side):
        return send(
            rows.at[cell, z, :, lanes(kind, side)],
            cols.at[core, z, high, i, :, lanes(kind, side)],
            cut_send.at[kind, z],
            cut_recv.at[kind, i],
            at(i, cell, high, core),
        )

    def cut_all(kind, side, local, remote):
        @pl.loop(0, 8)
        def _(n):
            j = (z + 4 + n) % 8
            itself = own_plane & (j == z)
            if local:

                @pl.when(itself)
                def _():
                    cut_local(j, kind, side).start()

            @pl.when(jnp.logical_not(itself))
            def _():
                remote(cut(j, kind, side))

    def on_side(side):
        return (cell // 4) == side

    factor = jnp.broadcast_to(10000.0 / total, (128, 256)).T
    inverse = 1.0 / jnp.maximum(width[...], 0.1)

    def standardize(first, last):
        factors = jnp.concatenate([factor] * ((last - first) // 128), axis=1)
        normal = jnp.log1p(raw[:, first:last] * factors)
        scaled = jnp.minimum((normal - centre[:, first:last]) * inverse[:, first:last], 10.0)
        rows[cell, :, :, first:last] = scaled.astype(BF16).reshape(8, 32, last - first)

    split = min(SHARED)
    for kind in (0, 1):
        if kind == 0:
            standardize(split, 512)
        else:
            standardize(0, split)
        if SHARED[0] == SHARED[1]:
            cut_all(kind, 0, True, lambda copy: copy.start())
        else:
            for side in (0, 1):

                @pl.when(on_side(side))
                def _():
                    cut_all(kind, side, True, lambda copy: copy.start())

    along = [((y + dy) % 4) * 2 + low for dy in (1, 3, 2)]

    def row_to(n, whose, target):
        return send(
            rows.at[whose], rows.at[whose], row_send.at[n], row_recv.at[whose],
            at(target, z, high, core),
        )

    row_copies = [row_to(0, cell, mirror)] + [
        row_to(1 + n, cell, c) for n, c in enumerate(along)
    ]
    for copy in row_copies:
        copy.start()

    out[...] = jnp.zeros_like(out)

    parts = [(s, k, side) for s, k in ((0, 0), (0, 1), (1, 1)) for side in (0, 1)]

    def place(q):
        return (z + PLACES[q]) % 8

    def view(j, whose, kind, side):
        return cols.at[core, j, whose, pl.ds(4 * side, 4), :, lanes(kind, side)]

    def piece(n, j):
        s, kind, side = parts[n]
        return view(j, other if s else high, kind, side)

    def ring(way, hop, n, j):
        ref = piece(n, j)
        return send(
            ref, ref, ring_send.at[way, hop, n], ring_recv.at[way, hop, n],
            (ahead, behind)[way],
        )

    def onward(way, hop, n):
        return ring(way, hop, n, (z + 8 - hop if way == 0 else z + hop) % 8)

    def arrival(way, hop, n):
        return ring(way, hop, n, (z + 7 - hop if way == 0 else z + 1 + hop) % 8)

    def swap(q, kind, side):
        ref = view(place(q), high, kind, side)
        return send(ref, ref, swap_send.at[kind, q, side], swap_recv.at[kind, q, side], partner)

    def swapped(q, kind, side):
        ref = view(place(q), other, kind, side)
        return send(ref, ref, swap_send.at[kind, q, side], swap_recv.at[kind, q, side], partner)

    def hand(q, s):
        ref = cols.at[core, place(q), other if s else high]
        return send(ref, ref, twin_send.at[q, s], twin_recv.at[q, s], twin)

    def handed(q, s):
        ref = cols.at[1 - core, place(q), other if s else high]
        return send(ref, ref, twin_send.at[q, s], twin_recv.at[q, s], twin)

    def last_hand(kind, side):
        ref = view(place(7), other, kind, side)
        return send(ref, ref, last_send.at[kind, side], last_recv.at[kind, side], twin)

    def last_handed(kind, side):
        ref = cols.at[1 - core, place(7), other, pl.ds(4 * side, 4), :, lanes(kind, side)]
        return send(ref, ref, last_send.at[kind, side], last_recv.at[kind, side], twin)

    def finish(q):
        for side in (0, 1):
            swapped(q, 0, side).wait_recv()
        hand(q, 1).start()

    def prepare(*qs):
        for q in qs:
            j = place(q)
            lhs[q] = jnp.concatenate([rows[i, j] for i in range(8)], axis=0).T

    def product(q, s, own, first=0, last=512):
        j, whose, which = place(q), other if s else high, core if own else 1 - core
        right = cols[which, j, whose, :, :, first:last].reshape(256, last - first)
        start = pl.multiple_of((whose * 2 + which) * 512 + first, 128)
        columns = pl.ds(start, last - first)
        out[:, columns] += jnp.dot(lhs[q], right, preferred_element_type=F32)

    def multiply(s, *qs):
        for q in qs:
            handed(q, s).wait_recv()
        whose = other if s else high

        @pl.loop(0, 2)
        def _(which):
            columns = pl.ds(pl.multiple_of((whose * 2 + which) * 512, 512), 512)
            right = [cols[which, place(q), whose].reshape(256, 512) for q in qs]
            left = [lhs[q] for q in qs]
            if len(qs) > 1:
                left, right = jnp.concatenate(left, axis=1), jnp.concatenate(right, axis=0)
            else:
                left, right = left[0], right[0]
            out[:, columns] += jnp.dot(left, right, preferred_element_type=F32)

    for kind in (0, 1):
        for side in (0, 1):
            for i in range(4 * side, 4 * side + 4):
                cut_from(i, kind, side).wait_recv()
            for way in (0, 1):
                onward(way, 0, 2 * kind + side).start()
            swap(0, kind, side).start()
    hand(0, 0).start()
    row_to(0, mirror, mirror).wait_recv()
    far_copies = [row_to(4 + n, mirror, c) for n, c in enumerate(along)]
    for copy in far_copies:
        copy.start()

    def begin_shared():
        for side in (0, 1):
            swapped(0, 1, side).wait_recv()
            for way in (0, 1):
                onward(way, 0, 4 + side).start()
        finish(0)

    def totals_left():
        @pl.loop(1, 32)
        def _(off):
            total_to(off).wait_send()

    def rows_arrive():
        for dy in (1, 2, 3):
            for l in (0, 1):
                c = ((y + dy) % 4) * 2 + l
                row_to(0, c, mirror).wait_recv()

    def cuts_left():
        for kind in (0, 1):
            if SHARED[0] == SHARED[1]:
                cut_all(kind, 0, False, lambda copy: copy.wait_send())
            else:
                for side in (0, 1):

                    @pl.when(on_side(side))
                    def _():
                        cut_all(kind, side, False, lambda copy: copy.wait_send())

    def rows_left():
        for copy in row_copies + far_copies:
            copy.wait_send()

    def ring_left(hop):
        for way in (0, 1):
            for n in range(6):
                if hop < 3 or parts[n][2] == way:
                    onward(way, hop, n).wait_send()

    def swaps_left(q):
        for side in (0, 1):
            swap(q, 0, side).wait_send()
        hand(q, 0).wait_send()
        if q < 7:
            hand(q, 1).wait_send()

    def last_swapped():
        for side in (0, 1):
            swapped(7, 0, side).wait_recv()
            last_hand(0, side).start()
        product(7, 0, True)
        product(7, 1, True, wide, 512)

    wide = max(SHARED)
    beside = {
        (0, 0): [],
        (1, 0): [begin_shared, cuts_left],
        (2, 0): [lambda: finish(1), lambda: finish(2)],
        (1, 1): [totals_left],
        (2, 1): [lambda: finish(3), lambda: finish(4), rows_arrive, lambda: prepare(0, 1, 2), lambda: multiply(0, 0, 1, 2)],
        (1, 2): [lambda: multiply(1, 0, 1, 2), lambda: prepare(3, 4)],
        (0, 3): [lambda: multiply(0, 3, 4), lambda: multiply(1, 3, 4), lambda: prepare(5, 6, 7)],
        (2, 2): [lambda: finish(5), lambda: finish(6), lambda: multiply(0, 5, 6), lambda: ring_left(0), rows_left],
        (1, 3): [lambda: multiply(1, 5, 6), last_swapped],
    }
    order = (
        (0, 0), (1, 0), (0, 1), (2, 0), (1, 1), (0, 2),
        (2, 1), (1, 2), (0, 3), (2, 2), (1, 3), (2, 3),
    )
    for p, hop in order:
        for side in (0, 1):
            n = 2 * p + side
            for way in (0, 1):
                if hop == 3 and side != way:
                    continue
                arrival(way, hop, n).wait_recv()
                if hop < 2 or (hop == 2 and side == way):
                    onward(way, hop + 1, n).start()
                if p == 0:
                    swap(7 if hop == 3 else 2 * hop + 1 + way, 0, side).start()
                if (p, hop) == (2, 3):
                    last_hand(1, side).start()
        if p == 1:
            for q in (7,) if hop == 3 else (2 * hop + 1, 2 * hop + 2):
                hand(q, 0).start()
        for action in beside.get((p, hop), ()):
            action()
    product(7, 1, True, 0, wide)
    handed(7, 0).wait_recv()
    product(7, 0, False)
    for side in (0, 1):
        last_handed(0, side).wait_recv()
    product(7, 1, False, wide, 512)
    for side in (0, 1):
        last_handed(1, side).wait_recv()
    product(7, 1, False, 0, wide)

    for kind in (0, 1):
        for side in (0, 1):
            last_hand(kind, side).wait_send()
    for side in (0, 1):
        swap(0, 1, side).wait_send()
    for q in range(8):
        swaps_left(q)
    for hop in (1, 2, 3):
        ring_left(hop)


def shards(counts, gene_mean, gene_std):
    dma = pltpu.SemaphoreType.DMA
    operands = counts, gene_mean.reshape(1, 512), gene_std.reshape(1, 512)
    operands = [pltpu.with_memory_space_constraint(a, pltpu.HBM) for a in operands]
    gram = pl.pallas_call(
        kernel,
        out_shape=jax.ShapeDtypeStruct((512, 2048), F32),
        in_specs=[pl.BlockSpec(memory_space=pltpu.HBM)] * 3,
        out_specs=pl.BlockSpec(memory_space=pltpu.VMEM),
        scratch_shapes=[
            pltpu.VMEM((256, 512), F32),
            pltpu.VMEM((1, 512), F32),
            pltpu.VMEM((1, 512), F32),
            pltpu.VMEM((1, 256), F32),
            pltpu.VMEM((32, 1, 256), F32),
            pltpu.VMEM((8, 8, 32, 512), BF16),
            pltpu.VMEM((2, 8, 2, 8, 32, 512), BF16),
            pltpu.VMEM((8, 512, 256), BF16),
            dma((3,)),
            dma((32,)),
            dma((32,)),
            dma((7,)),
            dma((8,)),
            dma((2, 8)),
            dma((2, 8)),
            dma((2, 4, 6)),
            dma((2, 4, 6)),
            dma((2, 8, 2)),
            dma((2, 8, 2)),
            dma((8, 2)),
            dma((8, 2)),
            dma((2, 2)),
            dma((2, 2)),
        ],
        compiler_params=pltpu.CompilerParams(
            collective_id=0, has_side_effects=True, vmem_limit_bytes=40 << 20
        ),
        cost_estimate=pl.CostEstimate(
            flops=2 * 512 * 2048 * 2048, bytes_accessed=5 << 20, transcendentals=1 << 17
        ),
    )(*operands)
    return gram * (1.0 / 2048)


def solution(mesh):
    placed = (P("cell", "gene"), P("gene"), P("gene"))
    return jax.shard_map(
        shards, mesh=mesh, in_specs=placed, out_specs=P("gene", "cell"), check_vma=False
    )
```

```python
import jax
import jax.numpy as jnp
from jax import lax
from jax.experimental import pallas as pl
from jax.experimental.pallas import tpu as pltpu
from jax.sharding import PartitionSpec as P

MESH = pl.DeviceIdType.MESH
BF16, F32 = jnp.bfloat16, jnp.float32
SHARED = (256, 256)
PLACES = (0, 7, 1, 6, 2, 5, 3, 4)


def kernel(
    counts, mean, std, out,
    raw, centre, width, part, libs, rows, cols, lhs,
    raw_sem, lib_send, lib_recv, row_send, row_recv, cut_send, cut_recv,
    ring_send, ring_recv, swap_send, swap_recv, twin_send, twin_recv, last_send, last_recv,
):
    cell, gene = lax.axis_index("cell"), lax.axis_index("gene")
    y, low = cell // 2, cell % 2
    z, high, core = gene // 4, (gene // 2) % 2, gene % 2
    other = 1 - high

    def at(cell_, z_, high_, core_):
        return (cell_, z_ * 4 + high_ * 2 + core_)

    def send(src, dst, send_sem, recv_sem, device):
        return pltpu.make_async_remote_copy(
            src_ref=src,
            dst_ref=dst,
            send_sem=send_sem,
            recv_sem=recv_sem,
            device_id=device,
            device_id_type=MESH,
        )

    ahead, behind = at(cell, (z + 1) % 8, high, core), at(cell, (z + 7) % 8, high, core)
    partner, twin = at(cell, z, other, core), at(cell, z, high, 1 - core)
    mirror = y * 2 + (1 - low)
    own_plane = cell == z

    fetches = [
        pltpu.make_async_copy(counts, raw, raw_sem.at[0]),
        pltpu.make_async_copy(mean, centre, raw_sem.at[1]),
        pltpu.make_async_copy(std, width, raw_sem.at[2]),
    ]
    for fetch in fetches:
        fetch.start()

    barrier = pltpu.get_barrier_semaphore()

    def greet(device):
        pl.semaphore_signal(barrier, inc=1, device_id=device, device_id_type=MESH)

    @pl.loop(0, 8)
    def _(n):
        @pl.when(jnp.logical_not(own_plane & (n == cell)))
        def _():
            greet(at(n, cell, high, core))

    def far_first(n):
        return 16 + ((n + 1) // 2) * (1 - 2 * (n % 2))

    @pl.loop(0, 31)
    def _(n):
        greet((cell, (gene + far_first(n)) % 32))

    greet(at(mirror, z, high, core))
    for dy in (1, 2, 3):
        greet(at(((y + dy) % 4) * 2 + low, z, high, core))

    for fetch in fetches:
        fetch.wait()
    sums = jnp.sum(raw[...], axis=1, keepdims=True)
    part[...] = jnp.broadcast_to(sums, (256, 128)).T[0:1, :]
    libs[gene] = part[...]

    pl.semaphore_wait(barrier, jnp.where(own_plane, 7 + 31 + 4, 8 + 31 + 4))

    def total_to(off):
        to = (gene + off) % 32
        return send(part, libs.at[gene], lib_send.at[off], lib_recv.at[gene], (cell, to))

    def total_from(off):
        of = (gene + off) % 32
        return send(part, libs.at[of], lib_send.at[off], lib_recv.at[of], (cell, of))

    @pl.loop(0, 31)
    def _(n):
        total_to(far_first(n)).start()

    @pl.loop(1, 32)
    def _(off):
        total_from(off).wait_recv()

    total = libs[0]
    for n in range(1, 32):
        total = total + libs[n]
    def lanes(kind, side):
        shared = SHARED[side]
        return pl.ds(shared, 512 - shared) if kind == 0 else pl.ds(0, shared)

    def cut(j, kind, side):
        return send(
            rows.at[cell, j, :, lanes(kind, side)],
            cols.at[core, j, high, cell, :, lanes(kind, side)],
            cut_send.at[kind, j],
            cut_recv.at[kind, cell],
            at(z, j, high, core),
        )

    def cut_local(j, kind, side):
        return pltpu.make_async_copy(
            rows.at[cell, j, :, lanes(kind, side)],
            cols.at[core, j, high, cell, :, lanes(kind, side)],
            cut_recv.at[kind, cell],
        )

    def cut_from(i, kind, side):
        return send(
            rows.at[cell, z, :, lanes(kind, side)],
            cols.at[core, z, high, i, :, lanes(kind, side)],
            cut_send.at[kind, z],
            cut_recv.at[kind, i],
            at(i, cell, high, core),
        )

    def cut_all(kind, side, local, remote):
        @pl.loop(0, 8)
        def _(n):
            j = (z + 4 + n) % 8
            itself = own_plane & (j == z)
            if local:

                @pl.when(itself)
                def _():
                    cut_local(j, kind, side).start()

            @pl.when(jnp.logical_not(itself))
            def _():
                remote(cut(j, kind, side))

    def on_side(side):
        return (cell // 4) == side

    factor = jnp.broadcast_to(10000.0 / total, (128, 256)).T
    inverse = 1.0 / jnp.maximum(width[...], 0.1)

    def standardize(first, last):
        factors = jnp.concatenate([factor] * ((last - first) // 128), axis=1)
        normal = jnp.log1p(raw[:, first:last] * factors)
        scaled = jnp.minimum((normal - centre[:, first:last]) * inverse[:, first:last], 10.0)
        rows[cell, :, :, first:last] = scaled.astype(BF16).reshape(8, 32, last - first)

    split = min(SHARED)
    for kind in (0, 1):
        if kind == 0:
            standardize(split, 512)
        else:
            standardize(0, split)
        if SHARED[0] == SHARED[1]:
            cut_all(kind, 0, True, lambda copy: copy.start())
        else:
            for side in (0, 1):

                @pl.when(on_side(side))
                def _():
                    cut_all(kind, side, True, lambda copy: copy.start())

    along = [((y + dy) % 4) * 2 + low for dy in (1, 3, 2)]

    def row_to(n, whose, target):
        return send(
            rows.at[whose], rows.at[whose], row_send.at[n], row_recv.at[whose],
            at(target, z, high, core),
        )

    row_copies = [row_to(0, cell, mirror)] + [
        row_to(1 + n, cell, c) for n, c in enumerate(along)
    ]
    for copy in row_copies:
        copy.start()

    out[...] = jnp.zeros_like(out)

    parts = [(s, k, side) for s, k in ((0, 0), (0, 1), (1, 1)) for side in (0, 1)]

    def place(q):
        return (z + PLACES[q]) % 8

    def view(j, whose, kind, side):
        return cols.at[core, j, whose, pl.ds(4 * side, 4), :, lanes(kind, side)]

    def piece(n, j):
        s, kind, side = parts[n]
        return view(j, other if s else high, kind, side)

    def ring(way, hop, n, j):
        ref = piece(n, j)
        return send(
            ref, ref, ring_send.at[way, hop, n], ring_recv.at[way, hop, n],
            (ahead, behind)[way],
        )

    def onward(way, hop, n):
        return ring(way, hop, n, (z + 8 - hop if way == 0 else z + hop) % 8)

    def arrival(way, hop, n):
        return ring(way, hop, n, (z + 7 - hop if way == 0 else z + 1 + hop) % 8)

    def swap(q, kind, side):
        ref = view(place(q), high, kind, side)
        return send(ref, ref, swap_send.at[kind, q, side], swap_recv.at[kind, q, side], partner)

    def swapped(q, kind, side):
        ref = view(place(q), other, kind, side)
        return send(ref, ref, swap_send.at[kind, q, side], swap_recv.at[kind, q, side], partner)

    def hand(q, s):
        ref = cols.at[core, place(q), other if s else high]
        return send(ref, ref, twin_send.at[q, s], twin_recv.at[q, s], twin)

    def handed(q, s):
        ref = cols.at[1 - core, place(q), other if s else high]
        return send(ref, ref, twin_send.at[q, s], twin_recv.at[q, s], twin)

    def last_hand(kind, side):
        ref = view(place(7), other, kind, side)
        return send(ref, ref, last_send.at[kind, side], last_recv.at[kind, side], twin)

    def last_handed(kind, side):
        ref = cols.at[1 - core, place(7), other, pl.ds(4 * side, 4), :, lanes(kind, side)]
        return send(ref, ref, last_send.at[kind, side], last_recv.at[kind, side], twin)

    def finish(q):
        for side in (0, 1):
            swapped(q, 0, side).wait_recv()
        hand(q, 1).start()

    def prepare(*qs):
        for q in qs:
            j = place(q)
            lhs[q] = jnp.concatenate([rows[i, j] for i in range(8)], axis=0).T

    def product(q, s, own, first=0, last=512):
        j, whose, which = place(q), other if s else high, core if own else 1 - core
        right = cols[which, j, whose, :, :, first:last].reshape(256, last - first)
        start = pl.multiple_of((whose * 2 + which) * 512 + first, 128)
        columns = pl.ds(start, last - first)
        out[:, columns] = (
            out[:, columns] + jnp.dot(lhs[q], right, preferred_element_type=F32)
        ) * (1.0 / 2048)

    def multiply(s, *qs):
        for q in qs:
            handed(q, s).wait_recv()
        whose = other if s else high

        @pl.loop(0, 2)
        def _(which):
            columns = pl.ds(pl.multiple_of((whose * 2 + which) * 512, 512), 512)
            right = [cols[which, place(q), whose].reshape(256, 512) for q in qs]
            left = [lhs[q] for q in qs]
            if len(qs) > 1:
                left, right = jnp.concatenate(left, axis=1), jnp.concatenate(right, axis=0)
            else:
                left, right = left[0], right[0]
            out[:, columns] += jnp.dot(left, right, preferred_element_type=F32)

    for kind in (0, 1):
        for side in (0, 1):
            for i in range(4 * side, 4 * side + 4):
                cut_from(i, kind, side).wait_recv()
            for way in (0, 1):
                onward(way, 0, 2 * kind + side).start()
            swap(0, kind, side).start()
    hand(0, 0).start()
    row_to(0, mirror, mirror).wait_recv()
    far_copies = [row_to(4 + n, mirror, c) for n, c in enumerate(along)]
    for copy in far_copies:
        copy.start()

    def begin_shared():
        for side in (0, 1):
            swapped(0, 1, side).wait_recv()
            for way in (0, 1):
                onward(way, 0, 4 + side).start()
        finish(0)

    def totals_left():
        @pl.loop(1, 32)
        def _(off):
            total_to(off).wait_send()

    def rows_arrive():
        for dy in (1, 2, 3):
            for l in (0, 1):
                c = ((y + dy) % 4) * 2 + l
                row_to(0, c, mirror).wait_recv()

    def cuts_left():
        for kind in (0, 1):
            if SHARED[0] == SHARED[1]:
                cut_all(kind, 0, False, lambda copy: copy.wait_send())
            else:
                for side in (0, 1):

                    @pl.when(on_side(side))
                    def _():
                        cut_all(kind, side, False, lambda copy: copy.wait_send())

    def rows_left():
        for copy in row_copies + far_copies:
            copy.wait_send()

    def ring_left(hop):
        for way in (0, 1):
            for n in range(6):
                if hop < 3 or parts[n][2] == way:
                    onward(way, hop, n).wait_send()

    def swaps_left(q):
        for side in (0, 1):
            swap(q, 0, side).wait_send()
        hand(q, 0).wait_send()
        if q < 7:
            hand(q, 1).wait_send()

    def early_left():
        ring_left(1)
        for side in (0, 1):
            swap(0, 1, side).wait_send()
        for q in range(5):
            swaps_left(q)

    def last_swapped():
        for side in (0, 1):
            swapped(7, 0, side).wait_recv()
            last_hand(0, side).start()
        product(7, 0, True)
        product(7, 1, True, wide, 512)

    wide = max(SHARED)
    beside = {
        (0, 0): [],
        (1, 0): [begin_shared, cuts_left],
        (2, 0): [lambda: finish(1), lambda: finish(2)],
        (1, 1): [totals_left],
        (2, 1): [lambda: finish(3), lambda: finish(4), rows_arrive, lambda: prepare(0, 1, 2), lambda: multiply(0, 0, 1, 2)],
        (1, 2): [lambda: multiply(1, 0, 1, 2), lambda: prepare(3, 4)],
        (0, 3): [lambda: multiply(0, 3, 4), lambda: multiply(1, 3, 4), lambda: prepare(5, 6, 7)],
        (2, 2): [lambda: finish(5), lambda: finish(6), lambda: multiply(0, 5, 6), lambda: ring_left(0), rows_left, early_left],
        (1, 3): [lambda: multiply(1, 5, 6), last_swapped],
    }
    order = (
        (0, 0), (1, 0), (0, 1), (2, 0), (1, 1), (0, 2),
        (2, 1), (1, 2), (0, 3), (2, 2), (1, 3), (2, 3),
    )
    for p, hop in order:
        for side in (0, 1):
            n = 2 * p + side
            for way in (0, 1):
                if hop == 3 and side != way:
                    continue
                arrival(way, hop, n).wait_recv()
                if hop < 2 or (hop == 2 and side == way):
                    onward(way, hop + 1, n).start()
                if p == 0:
                    swap(7 if hop == 3 else 2 * hop + 1 + way, 0, side).start()
                if (p, hop) == (2, 3):
                    last_hand(1, side).start()
        if p == 1:
            for q in (7,) if hop == 3 else (2 * hop + 1, 2 * hop + 2):
                hand(q, 0).start()
        for action in beside.get((p, hop), ()):
            action()
    product(7, 1, True, 0, wide)
    handed(7, 0).wait_recv()
    product(7, 0, False)
    for side in (0, 1):
        last_handed(0, side).wait_recv()
    product(7, 1, False, wide, 512)
    for side in (0, 1):
        last_handed(1, side).wait_recv()
    product(7, 1, False, 0, wide)

    for kind in (0, 1):
        for side in (0, 1):
            last_hand(kind, side).wait_send()
    for q in (5, 6, 7):
        swaps_left(q)
    for hop in (2, 3):
        ring_left(hop)


def shards(counts, gene_mean, gene_std):
    dma = pltpu.SemaphoreType.DMA
    operands = counts, gene_mean.reshape(1, 512), gene_std.reshape(1, 512)
    operands = [pltpu.with_memory_space_constraint(a, pltpu.HBM) for a in operands]
    gram = pl.pallas_call(
        kernel,
        out_shape=jax.ShapeDtypeStruct((512, 2048), F32),
        in_specs=[pl.BlockSpec(memory_space=pltpu.HBM)] * 3,
        out_specs=pl.BlockSpec(memory_space=pltpu.VMEM),
        scratch_shapes=[
            pltpu.VMEM((256, 512), F32),
            pltpu.VMEM((1, 512), F32),
            pltpu.VMEM((1, 512), F32),
            pltpu.VMEM((1, 256), F32),
            pltpu.VMEM((32, 1, 256), F32),
            pltpu.VMEM((8, 8, 32, 512), BF16),
            pltpu.VMEM((2, 8, 2, 8, 32, 512), BF16),
            pltpu.VMEM((8, 512, 256), BF16),
            dma((3,)),
            dma((32,)),
            dma((32,)),
            dma((7,)),
            dma((8,)),
            dma((2, 8)),
            dma((2, 8)),
            dma((2, 4, 6)),
            dma((2, 4, 6)),
            dma((2, 8, 2)),
            dma((2, 8, 2)),
            dma((8, 2)),
            dma((8, 2)),
            dma((2, 2)),
            dma((2, 2)),
        ],
        compiler_params=pltpu.CompilerParams(
            collective_id=0, has_side_effects=True, vmem_limit_bytes=40 << 20
        ),
        cost_estimate=pl.CostEstimate(
            flops=2 * 512 * 2048 * 2048, bytes_accessed=5 << 20, transcendentals=1 << 17
        ),
    )(*operands)

    def store(src, dst, sems):
        copies = [
            pltpu.make_async_copy(src.at[pl.ds(64 * n, 64)], dst.at[pl.ds(64 * n, 64)], sems.at[n])
            for n in range(8)
        ]
        for copy in copies:
            copy.start()
        for copy in copies:
            copy.wait()

    return pl.pallas_call(
        store,
        out_shape=jax.ShapeDtypeStruct((512, 2048), F32),
        in_specs=[pl.BlockSpec(memory_space=pltpu.VMEM)],
        out_specs=pl.BlockSpec(memory_space=pltpu.HBM),
        scratch_shapes=[dma((8,))],
        compiler_params=pltpu.CompilerParams(vmem_limit_bytes=8 << 20),
    )(gram)


def solution(mesh):
    placed = (P("cell", "gene"), P("gene"), P("gene"))
    return jax.shard_map(
        shards, mesh=mesh, in_specs=placed, out_specs=P("gene", "cell"), check_vma=False
    )
```

```python
import jax
import jax.numpy as jnp
from jax import lax
from jax.experimental import pallas as pl
from jax.experimental.pallas import tpu as pltpu
from jax.sharding import PartitionSpec as P

MESH = pl.DeviceIdType.MESH
BF16, F32 = jnp.bfloat16, jnp.float32
SHARED = (256, 256)
PLACES = (0, 7, 1, 6, 2, 5, 3, 4)


def kernel(
    counts, mean, std, out,
    raw, centre, width, part, libs, rows, cols, lhs,
    raw_sem, lib_send, lib_recv, row_send, row_recv, cut_send, cut_recv,
    ring_send, ring_recv, swap_send, swap_recv, twin_send, twin_recv, last_send, last_recv,
):
    cell, gene = lax.axis_index("cell"), lax.axis_index("gene")
    y, low = cell // 2, cell % 2
    z, high, core = gene // 4, (gene // 2) % 2, gene % 2
    other = 1 - high

    def at(cell_, z_, high_, core_):
        return (cell_, z_ * 4 + high_ * 2 + core_)

    def send(src, dst, send_sem, recv_sem, device):
        return pltpu.make_async_remote_copy(
            src_ref=src,
            dst_ref=dst,
            send_sem=send_sem,
            recv_sem=recv_sem,
            device_id=device,
            device_id_type=MESH,
        )

    ahead, behind = at(cell, (z + 1) % 8, high, core), at(cell, (z + 7) % 8, high, core)
    partner, twin = at(cell, z, other, core), at(cell, z, high, 1 - core)
    mirror = y * 2 + (1 - low)
    own_plane = cell == z

    fetches = [
        pltpu.make_async_copy(counts, raw, raw_sem.at[0]),
        pltpu.make_async_copy(mean, centre, raw_sem.at[1]),
        pltpu.make_async_copy(std, width, raw_sem.at[2]),
    ]
    for fetch in fetches:
        fetch.start()

    barrier = pltpu.get_barrier_semaphore()

    def greet(device):
        pl.semaphore_signal(barrier, inc=1, device_id=device, device_id_type=MESH)

    @pl.loop(0, 8)
    def _(n):
        @pl.when(jnp.logical_not(own_plane & (n == cell)))
        def _():
            greet(at(n, cell, high, core))

    def far_first(n):
        return 16 + ((n + 1) // 2) * (1 - 2 * (n % 2))

    @pl.loop(0, 31)
    def _(n):
        greet((cell, (gene + far_first(n)) % 32))

    greet(at(mirror, z, high, core))
    for dy in (1, 2, 3):
        greet(at(((y + dy) % 4) * 2 + low, z, high, core))

    for fetch in fetches:
        fetch.wait()
    sums = jnp.sum(raw[...], axis=1, keepdims=True)
    part[...] = jnp.broadcast_to(sums, (256, 128)).T[0:1, :]
    libs[gene] = part[...]

    pl.semaphore_wait(barrier, jnp.where(own_plane, 7 + 31 + 4, 8 + 31 + 4))

    def total_to(off):
        to = (gene + off) % 32
        return send(part, libs.at[gene], lib_send.at[off], lib_recv.at[gene], (cell, to))

    def total_from(off):
        of = (gene + off) % 32
        return send(part, libs.at[of], lib_send.at[off], lib_recv.at[of], (cell, of))

    @pl.loop(0, 31)
    def _(n):
        total_to(far_first(n)).start()

    @pl.loop(1, 32)
    def _(off):
        total_from(off).wait_recv()

    total = libs[0]
    for n in range(1, 32):
        total = total + libs[n]
    def lanes(kind, side):
        shared = SHARED[side]
        return pl.ds(shared, 512 - shared) if kind == 0 else pl.ds(0, shared)

    def cut(j, kind, side):
        return send(
            rows.at[cell, j, :, lanes(kind, side)],
            cols.at[core, j, high, cell, :, lanes(kind, side)],
            cut_send.at[kind, j],
            cut_recv.at[kind, cell],
            at(z, j, high, core),
        )

    def cut_local(j, kind, side):
        return pltpu.make_async_copy(
            rows.at[cell, j, :, lanes(kind, side)],
            cols.at[core, j, high, cell, :, lanes(kind, side)],
            cut_recv.at[kind, cell],
        )

    def cut_from(i, kind, side):
        return send(
            rows.at[cell, z, :, lanes(kind, side)],
            cols.at[core, z, high, i, :, lanes(kind, side)],
            cut_send.at[kind, z],
            cut_recv.at[kind, i],
            at(i, cell, high, core),
        )

    def cut_all(kind, side, local, remote):
        @pl.loop(0, 8)
        def _(n):
            j = (z + 4 + n) % 8
            itself = own_plane & (j == z)
            if local:

                @pl.when(itself)
                def _():
                    cut_local(j, kind, side).start()

            @pl.when(jnp.logical_not(itself))
            def _():
                remote(cut(j, kind, side))

    def on_side(side):
        return (cell // 4) == side

    factor = jnp.broadcast_to(10000.0 / total, (128, 256)).T
    inverse = 1.0 / jnp.maximum(width[...], 0.1)

    def standardize(first, last):
        factors = jnp.concatenate([factor] * ((last - first) // 128), axis=1)
        normal = jnp.log1p(raw[:, first:last] * factors)
        scaled = jnp.minimum((normal - centre[:, first:last]) * inverse[:, first:last], 10.0)
        rows[cell, :, :, first:last] = scaled.astype(BF16).reshape(8, 32, last - first)

    split = min(SHARED)
    for kind in (0, 1):
        if kind == 0:
            standardize(split, 512)
        else:
            standardize(0, split)
        if SHARED[0] == SHARED[1]:
            cut_all(kind, 0, True, lambda copy: copy.start())
        else:
            for side in (0, 1):

                @pl.when(on_side(side))
                def _():
                    cut_all(kind, side, True, lambda copy: copy.start())

    along = [((y + dy) % 4) * 2 + low for dy in (1, 3, 2)]

    def row_to(n, whose, target):
        return send(
            rows.at[whose], rows.at[whose], row_send.at[n], row_recv.at[whose],
            at(target, z, high, core),
        )

    row_copies = [row_to(0, cell, mirror)] + [
        row_to(1 + n, cell, c) for n, c in enumerate(along)
    ]
    for copy in row_copies:
        copy.start()

    out[...] = jnp.zeros_like(out)

    parts = [(s, k, side) for s, k in ((0, 0), (0, 1), (1, 1)) for side in (0, 1)]

    def place(q):
        return (z + PLACES[q]) % 8

    def view(j, whose, kind, side):
        return cols.at[core, j, whose, pl.ds(4 * side, 4), :, lanes(kind, side)]

    def piece(n, j):
        s, kind, side = parts[n]
        return view(j, other if s else high, kind, side)

    def ring(way, hop, n, j):
        ref = piece(n, j)
        return send(
            ref, ref, ring_send.at[way, hop, n], ring_recv.at[way, hop, n],
            (ahead, behind)[way],
        )

    def onward(way, hop, n):
        return ring(way, hop, n, (z + 8 - hop if way == 0 else z + hop) % 8)

    def arrival(way, hop, n):
        return ring(way, hop, n, (z + 7 - hop if way == 0 else z + 1 + hop) % 8)

    def swap(q, kind, side):
        ref = view(place(q), high, kind, side)
        return send(ref, ref, swap_send.at[kind, q, side], swap_recv.at[kind, q, side], partner)

    def swapped(q, kind, side):
        ref = view(place(q), other, kind, side)
        return send(ref, ref, swap_send.at[kind, q, side], swap_recv.at[kind, q, side], partner)

    def hand(q, s):
        ref = cols.at[core, place(q), other if s else high]
        return send(ref, ref, twin_send.at[q, s], twin_recv.at[q, s], twin)

    def handed(q, s):
        ref = cols.at[1 - core, place(q), other if s else high]
        return send(ref, ref, twin_send.at[q, s], twin_recv.at[q, s], twin)

    def last_hand(kind, side):
        ref = view(place(7), other, kind, side)
        return send(ref, ref, last_send.at[kind, side], last_recv.at[kind, side], twin)

    def last_handed(kind, side):
        ref = cols.at[1 - core, place(7), other, pl.ds(4 * side, 4), :, lanes(kind, side)]
        return send(ref, ref, last_send.at[kind, side], last_recv.at[kind, side], twin)

    def finish(q):
        for side in (0, 1):
            swapped(q, 0, side).wait_recv()
        hand(q, 1).start()

    def prepare(*qs):
        for q in qs:
            j = place(q)
            lhs[q] = jnp.concatenate([rows[i, j] for i in range(8)], axis=0).T

    def product(q, s, own, first=0, last=512):
        j, whose, which = place(q), other if s else high, core if own else 1 - core
        right = cols[which, j, whose, :, :, first:last].reshape(256, last - first)
        start = pl.multiple_of((whose * 2 + which) * 512 + first, 128)
        columns = pl.ds(start, last - first)
        out[:, columns] = (
            out[:, columns] + jnp.dot(lhs[q], right, preferred_element_type=F32)
        ) * (1.0 / 2048)

    def multiply(s, *qs):
        for q in qs:
            handed(q, s).wait_recv()
        whose = other if s else high

        @pl.loop(0, 2)
        def _(which):
            columns = pl.ds(pl.multiple_of((whose * 2 + which) * 512, 512), 512)
            right = [cols[which, place(q), whose].reshape(256, 512) for q in qs]
            left = [lhs[q] for q in qs]
            if len(qs) > 1:
                left, right = jnp.concatenate(left, axis=1), jnp.concatenate(right, axis=0)
            else:
                left, right = left[0], right[0]
            out[:, columns] += jnp.dot(left, right, preferred_element_type=F32)

    for kind in (0, 1):
        for side in (0, 1):
            for i in range(4 * side, 4 * side + 4):
                cut_from(i, kind, side).wait_recv()
            for way in (0, 1):
                onward(way, 0, 2 * kind + side).start()
            swap(0, kind, side).start()
    hand(0, 0).start()
    row_to(0, mirror, mirror).wait_recv()
    far_copies = [row_to(4 + n, mirror, c) for n, c in enumerate(along)]
    for copy in far_copies:
        copy.start()

    def begin_shared():
        for side in (0, 1):
            swapped(0, 1, side).wait_recv()
            for way in (0, 1):
                onward(way, 0, 4 + side).start()
        finish(0)

    def totals_left():
        @pl.loop(1, 32)
        def _(off):
            total_to(off).wait_send()

    def rows_arrive():
        for dy in (1, 2, 3):
            for l in (0, 1):
                c = ((y + dy) % 4) * 2 + l
                row_to(0, c, mirror).wait_recv()

    def cuts_left():
        for kind in (0, 1):
            if SHARED[0] == SHARED[1]:
                cut_all(kind, 0, False, lambda copy: copy.wait_send())
            else:
                for side in (0, 1):

                    @pl.when(on_side(side))
                    def _():
                        cut_all(kind, side, False, lambda copy: copy.wait_send())

    def rows_left():
        for copy in row_copies + far_copies:
            copy.wait_send()

    def ring_left(hop):
        for way in (0, 1):
            for n in range(6):
                if hop < 3 or parts[n][2] == way:
                    onward(way, hop, n).wait_send()

    def swaps_left(q):
        for side in (0, 1):
            swap(q, 0, side).wait_send()
        hand(q, 0).wait_send()
        if q < 7:
            hand(q, 1).wait_send()

    def early_left():
        ring_left(1)
        for side in (0, 1):
            swap(0, 1, side).wait_send()
        for q in range(5):
            swaps_left(q)

    def last_swapped():
        for side in (0, 1):
            swapped(7, 0, side).wait_recv()
            last_hand(0, side).start()
        product(7, 0, True)
        product(7, 1, True, wide, 512)
        handed(7, 0).wait_recv()
        product(7, 0, False)

    wide = max(SHARED)
    beside = {
        (0, 0): [],
        (1, 0): [begin_shared, cuts_left],
        (2, 0): [lambda: finish(1), lambda: finish(2)],
        (1, 1): [totals_left],
        (2, 1): [lambda: finish(3), lambda: finish(4), rows_arrive, lambda: prepare(0, 1, 2), lambda: multiply(0, 0, 1, 2)],
        (1, 2): [lambda: multiply(1, 0, 1, 2), lambda: prepare(3, 4)],
        (0, 3): [lambda: multiply(0, 3, 4), lambda: multiply(1, 3, 4), lambda: prepare(5, 6, 7)],
        (2, 2): [lambda: finish(5), lambda: finish(6), lambda: multiply(0, 5, 6), lambda: ring_left(0), rows_left, early_left],
        (1, 3): [lambda: multiply(1, 5, 6), last_swapped],
    }
    order = (
        (0, 0), (1, 0), (0, 1), (2, 0), (1, 1), (0, 2),
        (2, 1), (1, 2), (0, 3), (2, 2), (1, 3), (2, 3),
    )
    for p, hop in order:
        for side in (0, 1):
            n = 2 * p + side
            for way in (0, 1):
                if hop == 3 and side != way:
                    continue
                arrival(way, hop, n).wait_recv()
                if hop < 2 or (hop == 2 and side == way):
                    onward(way, hop + 1, n).start()
                if p == 0:
                    swap(7 if hop == 3 else 2 * hop + 1 + way, 0, side).start()
                if (p, hop) == (2, 3):
                    last_hand(1, side).start()
        if p == 1:
            for q in (7,) if hop == 3 else (2 * hop + 1, 2 * hop + 2):
                hand(q, 0).start()
        for action in beside.get((p, hop), ()):
            action()
    product(7, 1, True, 0, wide)
    for side in (0, 1):
        last_handed(0, side).wait_recv()
    product(7, 1, False, wide, 512)
    for side in (0, 1):
        last_handed(1, side).wait_recv()
    product(7, 1, False, 0, wide)

    for kind in (0, 1):
        for side in (0, 1):
            last_hand(kind, side).wait_send()
    for q in (5, 6, 7):
        swaps_left(q)
    for hop in (2, 3):
        ring_left(hop)


def shards(counts, gene_mean, gene_std):
    dma = pltpu.SemaphoreType.DMA
    operands = counts, gene_mean.reshape(1, 512), gene_std.reshape(1, 512)
    operands = [pltpu.with_memory_space_constraint(a, pltpu.HBM) for a in operands]
    gram = pl.pallas_call(
        kernel,
        out_shape=jax.ShapeDtypeStruct((512, 2048), F32),
        in_specs=[pl.BlockSpec(memory_space=pltpu.HBM)] * 3,
        out_specs=pl.BlockSpec(memory_space=pltpu.VMEM),
        scratch_shapes=[
            pltpu.VMEM((256, 512), F32),
            pltpu.VMEM((1, 512), F32),
            pltpu.VMEM((1, 512), F32),
            pltpu.VMEM((1, 256), F32),
            pltpu.VMEM((32, 1, 256), F32),
            pltpu.VMEM((8, 8, 32, 512), BF16),
            pltpu.VMEM((2, 8, 2, 8, 32, 512), BF16),
            pltpu.VMEM((8, 512, 256), BF16),
            dma((3,)),
            dma((32,)),
            dma((32,)),
            dma((7,)),
            dma((8,)),
            dma((2, 8)),
            dma((2, 8)),
            dma((2, 4, 6)),
            dma((2, 4, 6)),
            dma((2, 8, 2)),
            dma((2, 8, 2)),
            dma((8, 2)),
            dma((8, 2)),
            dma((2, 2)),
            dma((2, 2)),
        ],
        compiler_params=pltpu.CompilerParams(
            collective_id=0, has_side_effects=True, vmem_limit_bytes=40 << 20
        ),
        cost_estimate=pl.CostEstimate(
            flops=2 * 512 * 2048 * 2048, bytes_accessed=5 << 20, transcendentals=1 << 17
        ),
    )(*operands)

    def store(src, dst, sems):
        copies = [
            pltpu.make_async_copy(src.at[pl.ds(64 * n, 64)], dst.at[pl.ds(64 * n, 64)], sems.at[n])
            for n in range(8)
        ]
        for copy in copies:
            copy.start()
        for copy in copies:
            copy.wait()

    return pl.pallas_call(
        store,
        out_shape=jax.ShapeDtypeStruct((512, 2048), F32),
        in_specs=[pl.BlockSpec(memory_space=pltpu.VMEM)],
        out_specs=pl.BlockSpec(memory_space=pltpu.HBM),
        scratch_shapes=[dma((8,))],
        compiler_params=pltpu.CompilerParams(vmem_limit_bytes=8 << 20),
    )(gram)


def solution(mesh):
    placed = (P("cell", "gene"), P("gene"), P("gene"))
    return jax.shard_map(
        shards, mesh=mesh, in_specs=placed, out_specs=P("gene", "cell"), check_vma=False
    )
```
